32 devices in a mesh: epoch: 2 (over x), tile: 16 (over z, y, core).
Axes of the slice: x: 2, y: 2, z: 4, core: 2. Of those that a mesh axis runs over, the one named last changes fastest.
Arguments:
- owners: int32 [2, 2048], P('epoch', 'tile'), may hold values from 0 to 15, as said below
- row_offsets: int32 [2, 2048], P('epoch', 'tile'), may hold values from 0 to 224
- col_offsets: int32 [2, 2048], P('epoch', 'tile'), may hold values from 0 to 4064
- samples: bfloat16 [2, 2048, 2, 256], P('epoch', 'tile'), may hold values from -6 to 6
- coords: float32 [2, 2048, 2, 256], P('epoch', 'tile'), may hold values from 4 to 28
- taper_rows: float32 [16, 256], P('epoch'), may hold values from 1 to 4
- taper_cols: float32 [4096], P('tile'), may hold values from 1 to 4
Outputs:
- image: float32 [16, 256, 4096], P('epoch', None, 'tile')
The draws below stay inside these ranges and needn't reach their ends.
Inputs may be any that keep to these rules, and one draw needn't show every extreme that they name: `owners`: in every epoch, within each aligned block of 128 slots (the slots of one index of tile), no owner tile is named more than 10 times, and one owner tile is named exactly 10 times in every block of that epoch.
All inputs are finite; a program needn't handle non-finite values.
Results may differ from the reference program's by a relative error of at most 0.0053.
Values may be sent and summed in bfloat16 or wider, within the bound.
A program may use at most 128 MiB of HBM per device.

```python
import math
import jax
import jax.numpy as jnp
from jax import lax

G = 4096
SUB = 32
NK = 256
S_DEV = 128
EPOCHS = 2
TILES = 16
SLOTS = 2048
CAP = 10
BAND = 256


def draw_owners(key, part):
    key_level, key_hot, key_noise, key_order = jax.random.split(key, 4)
    pool_size = TILES * CAP
    level = jax.random.randint(key_level, (EPOCHS, TILES), 0, 4, dtype=jnp.int32)
    hot_tile = jax.random.randint(key_hot, (EPOCHS,), 0, TILES, dtype=jnp.int32)
    cand_owner = jnp.arange(pool_size, dtype=jnp.int32) // CAP
    boost = level[:, cand_owner] + 4 * (cand_owner[None, :] == hot_tile[:, None]).astype(jnp.int32)
    noise = jax.random.randint(key_noise, (EPOCHS, TILES, pool_size), 0, 65536, dtype=jnp.int32)
    scores = (boost[:, None, :] * 65536 + noise) * pool_size + jnp.arange(pool_size, dtype=jnp.int32)[None, None, :]
    top_values, chosen = lax.top_k(scores, S_DEV)
    picked = (chosen // CAP).astype(jnp.int32)
    order_keys = jax.random.randint(key_order, (EPOCHS, TILES, S_DEV), 0, 65536, dtype=jnp.int32) * S_DEV + jnp.arange(S_DEV, dtype=jnp.int32)[None, None, :]
    order = jnp.argsort(order_keys, axis=-1)
    shuffled = jnp.take_along_axis(picked, order, axis=-1)
    return shuffled.reshape(EPOCHS, TILES * S_DEV).astype(jnp.int32)


def with_ends(array, rng, least, largest):
    index_at = [jax.random.randint(jax.random.fold_in(rng, axis), (), 0, length) for axis, length in enumerate(array.shape)]
    longest = array.shape.index(max(array.shape))
    beside = index_at[:longest] + [(index_at[longest] + 1) % array.shape[longest]] + index_at[longest + 1:]
    return array.at[tuple(index_at)].set(least).at[tuple(beside)].set(largest)


def block_levels(key, dims, pieces, smallest, top_value):
    gain = 1.0
    for dim, blocks in pieces:
        draws = jax.random.uniform(jax.random.fold_in(jax.random.fold_in(key, 6), dim), (blocks,), jnp.float32, smallest / len(pieces), top_value / len(pieces))
        gain = gain * jnp.repeat(jnp.exp(draws), dims[dim] // blocks).reshape((-1,) + (1,) * (len(dims) - 1 - dim))
    return gain


def normal_values(rng, extent, deviation, limit, shards=(), kind=jnp.bfloat16):
    gain = block_levels(rng, extent, shards, -0.22, 0.18) if shards else 1.0
    values = jax.random.normal(rng, extent, jnp.float32) * deviation * gain
    return jnp.minimum(jnp.maximum(values, -limit), limit).astype(kind)


def setup_inputs(seed: int = 0) -> dict:
    streams_of = jax.random.split(jax.random.key(seed), 8)
    owners = draw_owners(jax.random.fold_in(streams_of[7], 71), 0)
    row_offsets = with_ends(jax.random.randint(streams_of[1], (EPOCHS, SLOTS), 0, BAND - SUB + 1), jax.random.fold_in(streams_of[1], 1), 0, BAND - SUB).astype(jnp.int32)
    col_offsets = with_ends(jax.random.randint(streams_of[2], (EPOCHS, SLOTS), 0, G - SUB + 1), jax.random.fold_in(streams_of[2], 1), 0, G - SUB).astype(jnp.int32)
    samples = normal_values(streams_of[3], (EPOCHS, SLOTS, 2, NK), 1.0, 6.0, ((0, 2), (1, 16)))
    coords = jnp.clip(4.0 + 24.0 * jax.random.uniform(streams_of[4], (EPOCHS, SLOTS, 2, NK), jnp.float32) ** block_levels(streams_of[4], (EPOCHS, SLOTS, 2, NK), ((0, 2), (1, 16)), -0.2, 0.2), 4.0, 28.0)
    taper_rows = jnp.clip(jnp.exp(math.log(4.0) - 1.3862944 * jax.random.uniform(streams_of[5], (TILES, BAND), jnp.float32) ** block_levels(streams_of[5], (TILES, BAND), ((0, 2),), -0.2, 0.2)), 1.0, 4.0)
    taper_cols = jnp.clip(jnp.exp(math.log(4.0) - 1.3862944 * jax.random.uniform(streams_of[6], (G,), jnp.float32) ** block_levels(streams_of[6], (G,), ((0, 16),), -0.2, 0.2)), 1.0, 4.0)
    return {"owners": owners, "row_offsets": row_offsets, "col_offsets": col_offsets, "samples": samples, "coords": coords, "taper_rows": taper_rows, "taper_cols": taper_cols}


def kernel_weights(distance):
    return jnp.square(jnp.maximum(1.0 - jnp.square(distance * 0.25), 0.0))

def grid_block(block_samples, block_coords):
    cell_pos = jnp.arange(SUB, dtype=jnp.float32)
    along_u = kernel_weights(cell_pos[None, :, None] - block_coords[:, 0, None, :]).astype(jnp.bfloat16)
    along_v = kernel_weights(cell_pos[None, None, :] - block_coords[:, 1, :, None])
    weighted = (jnp.transpose(block_samples, (0, 2, 1)).astype(jnp.float32)[:, :, :, None] * along_v[:, :, None, :]).astype(jnp.bfloat16)
    weighted = weighted.reshape(block_samples.shape[0], block_samples.shape[2], 2 * SUB)
    return jnp.einsum('sxk,skz->sxz', along_u.astype(jnp.float32), weighted.astype(jnp.float32)).astype(jnp.bfloat16)

def reference(owners, row_offsets, col_offsets, samples, coords, taper_rows, taper_cols):
    total = jnp.zeros((G * 2 * G,), jnp.float32)
    cell_steps = jnp.arange(SUB, dtype=jnp.int32)
    part_steps = jnp.arange(2, dtype=jnp.int32)
    for epoch_num in range(EPOCHS):
        epoch_samples = samples[epoch_num].reshape(TILES, S_DEV, 2, NK)
        epoch_coords = coords[epoch_num].reshape(TILES, S_DEV, 2, NK)
        subgrids = lax.map(lambda pair: grid_block(pair[0], pair[1]), (epoch_samples, epoch_coords))
        subgrids = subgrids.reshape(SLOTS, SUB, 2, SUB)
        slot_owner = owners[epoch_num].astype(jnp.int32)
        counts = jnp.zeros((TILES,), jnp.float32).at[slot_owner].add(1.0)
        weight = 1.0 / counts[slot_owner]
        row_index = (slot_owner * BAND + row_offsets[epoch_num]).astype(jnp.int32)[:, None] + cell_steps[None, :]
        col_index = col_offsets[epoch_num].astype(jnp.int32)[:, None] + cell_steps[None, :]
        flat_index = (row_index[:, :, None, None] * 2 + part_steps[None, None, :, None]) * G + col_index[:, None, None, :]
        values = subgrids.astype(jnp.float32) * weight[:, None, None, None]
        band_grid = jnp.zeros((G * 2 * G,), jnp.float32).at[flat_index.reshape(-1)].add(values.reshape(-1))
        rounded = lax.optimization_barrier(band_grid.astype(jnp.bfloat16)).astype(jnp.float32)
        total = total + rounded
    grid = total.reshape(G, 2, G)
    complex_grid = lax.complex(grid[:, 0, :], grid[:, 1, :])
    score_sum = jnp.real(jnp.fft.ifft2(complex_grid)) * float(G * G)
    reordered = score_sum.reshape(G, BAND, TILES).transpose(0, 2, 1).reshape(G, G)
    arranged = reordered.reshape(BAND, TILES, G).transpose(1, 0, 2)
    image_scale = math.sqrt(S_DEV) / (64.0 * TILES * math.sqrt(EPOCHS))
    result = arranged * image_scale * taper_rows[:, :, None] * taper_cols[None, None, :]
    return result.astype(jnp.float32)
```

```python
import math

import jax
import jax.numpy as jnp
from jax import lax
from jax.sharding import PartitionSpec as P

SUB = 32


def kernel_weights(distance):
    return jnp.square(jnp.maximum(1.0 - jnp.square(distance * 0.25), 0.0))


def grid_slots(slot_samples, slot_coords, sub_size):
    slot_total = slot_samples.shape[0]
    sample_count = slot_samples.shape[2]
    block_size = math.gcd(slot_total, 64)
    cell_pos = jnp.arange(sub_size, dtype=jnp.float32)

    def grid_block(pair):
        block_samples, block_coords = pair
        along_u = kernel_weights(cell_pos[None, :, None] - block_coords[:, 0, None, :]).astype(
            jnp.bfloat16
        )
        along_v = kernel_weights(cell_pos[None, None, :] - block_coords[:, 1, :, None])
        weighted = (
            jnp.transpose(block_samples, (0, 2, 1)).astype(jnp.float32)[:, :, :, None]
            * along_v[:, :, None, :]
        ).astype(jnp.bfloat16)
        weighted = weighted.reshape(block_size, sample_count, 2 * sub_size)
        return jnp.einsum(
            "sxk,skz->sxz", along_u, weighted, preferred_element_type=jnp.float32
        ).astype(jnp.bfloat16)

    grouped = (
        slot_samples.reshape(slot_total // block_size, block_size, 2, sample_count),
        slot_coords.reshape(slot_total // block_size, block_size, 2, sample_count),
    )
    return lax.map(grid_block, grouped).reshape(slot_total, sub_size, 2 * sub_size)


def make_table(out_count, in_count, modulus):
    out_idx = jnp.arange(out_count, dtype=jnp.int32)[:, None]
    in_idx = jnp.arange(in_count, dtype=jnp.int32)[None, :]
    angles = (out_idx * in_idx % modulus).astype(jnp.float32) * (2.0 * math.pi / modulus)
    cosine = jnp.cos(angles)
    sine = jnp.sin(angles)
    upper = jnp.stack([cosine, -sine], -1)
    lower = jnp.stack([sine, cosine], -1)
    return jnp.stack([upper, lower], 1)


def final_table(out_count, in_values, modulus):
    out_idx = jnp.arange(out_count, dtype=jnp.int32)[:, None]
    angles = (out_idx * in_values[None, :] % modulus).astype(jnp.float32) * (
        2.0 * math.pi / modulus
    )
    return jnp.stack([jnp.cos(angles), -jnp.sin(angles)], -1)


def rotate(real_part, imag_part, angles):
    cosine = jnp.cos(angles)
    sine = jnp.sin(angles)
    return (real_part * cosine - imag_part * sine, real_part * sine + imag_part * cosine)


def row_transform(band_part, grid_size, tile_count):
    rows_here = band_part.shape[0]
    band_len = grid_size // tile_count
    split_rows = band_part.reshape(rows_here, 2, tile_count, band_len)
    section_one = jnp.einsum(
        "mpaq,rqab->rmpb",
        make_table(tile_count, tile_count, tile_count),
        split_rows,
        precision=lax.Precision.HIGHEST,
    )
    first_idx = jnp.arange(tile_count, dtype=jnp.int32)[:, None]
    second_idx = jnp.arange(band_len, dtype=jnp.int32)[None, :]
    angles = (first_idx * second_idx % grid_size).astype(jnp.float32) * (2.0 * math.pi / grid_size)
    turned_re, turned_im = rotate(section_one[:, :, 0, :], section_one[:, :, 1, :], angles[None])
    turned = jnp.stack([turned_re, turned_im], 2)
    section_two = jnp.einsum(
        "npbq,rmqb->rpmn",
        make_table(band_len, band_len, band_len),
        turned,
        precision=lax.Precision.HIGHEST,
    )
    return section_two.reshape(rows_here, 2, grid_size)


def place_subgrids(received, info, band_rows, grid_size, sub_size):
    pool_size = received.shape[0]
    lane_blocks = grid_size // 128
    cell_steps = jnp.arange(sub_size, dtype=jnp.int32)
    col_block = info[:, 2] // 128
    col_start = info[:, 2] % 128
    window_pos = jnp.arange(256, dtype=jnp.int32)
    window_sel = (
        window_pos[None, None, :] == (col_start[:, None] + cell_steps[None, :])[:, :, None]
    ).astype(jnp.bfloat16)
    split_parts = received.reshape(pool_size, sub_size * 2, sub_size)
    windows = jnp.einsum(
        "sqy,syw->sqw", split_parts, window_sel, preferred_element_type=jnp.float32
    )
    windows = windows.reshape(pool_size, sub_size, 2, 2, 128).transpose(0, 1, 3, 2, 4)
    halves = jnp.arange(2, dtype=jnp.int32)
    target_block = col_block[:, None, None] + halves[None, None, :]
    target_row = info[:, 1][:, None, None] + cell_steps[None, :, None]
    target = target_row * lane_blocks + target_block
    target = jnp.where(target_block < lane_blocks, target, band_rows * lane_blocks)
    flat_band = jnp.zeros((band_rows * lane_blocks, 2, 128), jnp.float32)
    flat_band = flat_band.at[target.reshape(-1)].add(windows.reshape(-1, 2, 128), mode="drop")
    return (
        flat_band.reshape(band_rows, lane_blocks, 2, 128)
        .transpose(0, 2, 1, 3)
        .reshape(band_rows, 2, grid_size)
    )


def body(owners, row_offsets, col_offsets, samples, coords, taper_rows, taper_cols):
    tile_count = lax.axis_size("tile")
    epoch_count = lax.axis_size("epoch")
    epoch_index = lax.axis_index("epoch")
    slot_owner = owners[0]
    n_slots = slot_owner.shape[0]
    capacity = max(2, n_slots * 5 // (4 * tile_count))
    pool_size = tile_count * capacity
    band_rows = taper_cols.shape[0]
    grid_size = band_rows * tile_count
    band_dev = band_rows // epoch_count
    sub_size = SUB
    slot_idx = jnp.arange(n_slots, dtype=jnp.int32)
    same_before = (slot_owner[:, None] == slot_owner[None, :]) & (
        slot_idx[None, :] < slot_idx[:, None]
    )
    slot_rank = jnp.sum(same_before.astype(jnp.int32), 1)
    slot_dest = slot_owner * capacity + slot_rank
    slot_info = jnp.stack([jnp.ones_like(slot_owner), row_offsets[0], col_offsets[0]], 1)
    info_buffer = (
        jnp.zeros((pool_size, 3), jnp.int32)
        .at[slot_dest]
        .set(slot_info)
        .reshape(tile_count, capacity, 3)
    )
    subgrids = grid_slots(samples[0], coords[0], sub_size)
    packed = (
        jnp.zeros((pool_size, 2 * sub_size * sub_size), jnp.bfloat16)
        .at[slot_dest]
        .set(subgrids.reshape(n_slots, -1))
    )
    got_grids, got_info = (
        lax.all_to_all(
            packed.reshape(tile_count, capacity, -1),
            "tile",
            split_axis=0,
            concat_axis=0,
            tiled=True,
        ),
        lax.all_to_all(info_buffer, "tile", split_axis=0, concat_axis=0, tiled=True),
    )
    received = got_grids.reshape(pool_size, sub_size, 2 * sub_size)
    info = got_info.reshape(pool_size, 3)
    slot_count = jnp.sum(info[:, 0]).astype(jnp.float32)
    weight = 1.0 / jnp.maximum(slot_count, 1.0)
    band_grid = place_subgrids(received, info, band_rows, grid_size, sub_size) * weight
    summed = lax.psum_scatter(
        band_grid.astype(jnp.bfloat16), "epoch", scatter_dimension=0, tiled=True
    ).astype(jnp.float32)
    transformed = row_transform(summed, grid_size, tile_count).reshape(
        band_dev, 2, tile_count, band_rows
    )
    column_table = make_table(tile_count, tile_count, tile_count)
    gathered = lax.all_to_all(transformed, "tile", split_axis=2, concat_axis=0, tiled=True)
    item_count = gathered.shape[3]
    blocks = gathered.reshape(tile_count, band_dev, 2, item_count)
    mixed = jnp.einsum("cptq,trqm->crpm", column_table, blocks, precision=lax.Precision.HIGHEST)
    first_idx = jnp.arange(tile_count, dtype=jnp.int32)[:, None]
    row_global = epoch_index * band_dev + jnp.arange(band_dev, dtype=jnp.int32)[None, :]
    angles = (first_idx * row_global % grid_size).astype(jnp.float32) * (2.0 * math.pi / grid_size)
    turned_re, turned_im = rotate(mixed[:, :, 0, :], mixed[:, :, 1, :], angles[:, :, None])
    partial_rows = jnp.stack([turned_re, turned_im], 2)
    local_rows = epoch_index * band_dev + jnp.arange(band_dev, dtype=jnp.int32)
    local_table = final_table(band_rows, local_rows, band_rows)
    image_sum = lax.psum_scatter(
        jnp.einsum("trq,crqm->ctm", local_table, partial_rows, precision=lax.Precision.HIGHEST),
        "epoch",
        scatter_dimension=0,
        tiled=True,
    )
    image_scale = math.sqrt(n_slots) / (64.0 * tile_count * math.sqrt(epoch_count))
    result = image_sum * image_scale * taper_rows[:, :, None] * taper_cols[None, None, :]
    return result


def solution(mesh):
    placed = (
        P("epoch", "tile"),
        P("epoch", "tile"),
        P("epoch", "tile"),
        P("epoch", "tile", None, None),
        P("epoch", "tile", None, None),
        P("epoch", None),
        P("tile"),
    )
    return jax.shard_map(
        body, mesh=mesh, in_specs=placed, out_specs=P("epoch", None, "tile"), check_vma=False
    )
```

```python
import functools
import math

import jax
import jax.numpy as jnp
import numpy as np
from jax import lax
from jax.experimental import pallas as pl
from jax.experimental.pallas import tpu as pltpu
from jax.sharding import PartitionSpec as P

SUB = 32
LANES = 128
VMEM_BYTES = 56 * 1024 * 1024


def kernel_weights(distance):
    return jnp.square(jnp.maximum(1.0 - jnp.square(distance * 0.25), 0.0))


def fourier(values):
    count = len(values)
    if count == 1:
        return values
    if count == 2:
        (ar, ai), (br, bi) = values
        return [(ar + br, ai + bi), (ar - br, ai - bi)]
    even, odd = fourier(values[0::2]), fourier(values[1::2])
    low, high = [], []
    for k in range(count // 2):
        (er, ei), (orr, oi) = even[k], odd[k]
        if k == 0:
            tr, ti = orr, oi
        elif 4 * k == count:
            tr, ti = -oi, orr
        elif 8 * k == count:
            s = math.sqrt(0.5)
            tr, ti = (orr - oi) * s, (orr + oi) * s
        elif 8 * k == 3 * count:
            s = math.sqrt(0.5)
            tr, ti = (orr + oi) * -s, (orr - oi) * s
        else:
            c, s = math.cos(2 * math.pi * k / count), math.sin(2 * math.pi * k / count)
            tr, ti = orr * c - oi * s, orr * s + oi * c
        low.append((er + tr, ei + ti))
        high.append((er - tr, ei - ti))
    return low + high


def grid_kernel(pairs, src_ref, data_ref, info_ref, out_ref):
    cells = lax.broadcasted_iota(jnp.int32, (SUB, data_ref.shape[2]), 0).astype(jnp.float32)

    def one(slot):
        data = data_ref[slot]
        along_u = kernel_weights(cells - data[0:1]).astype(jnp.bfloat16)
        along_v = kernel_weights(cells - data[1:2])
        weighted = jnp.concatenate([data[2:3] * along_v, data[3:4] * along_v], 0)
        return lax.dot_general(
            along_u,
            weighted.astype(jnp.bfloat16),
            (((1,), (1,)), ((), ())),
            preferred_element_type=jnp.float32,
        )

    def per_tile(tile, carry):
        for k in range(pairs):
            at = (tile * pairs + k) * 2
            both = jnp.concatenate([one(src_ref[at]), one(src_ref[at + 1])], 1)
            out_ref[tile, k * SUB : (k + 1) * SUB, :] = both.astype(jnp.bfloat16)
        out_ref[tile, pairs * SUB :, :] = info_ref[tile]
        return carry

    lax.fori_loop(0, out_ref.shape[0], per_tile, 0)


def place_kernel(
    pairs, tile_count, row_ref, block_ref, start_ref, weight_ref, pool_ref, cos_ref, sin_ref, out_ref, acc
):
    lane_blocks, acc_rows = acc.shape[1], acc.shape[2]
    rows_out = out_ref.shape[1]
    block_len = out_ref.shape[2] // 2

    def clear(i, carry):
        acc[0, i] = jnp.zeros((acc_rows, LANES), jnp.float32)
        acc[1, i] = jnp.zeros((acc_rows, LANES), jnp.float32)
        return carry

    lax.fori_loop(0, lane_blocks, clear, 0)
    shape = (SUB, 2 * LANES)
    steps = lax.broadcasted_iota(jnp.int32, shape, 1) - lax.broadcasted_iota(jnp.int32, shape, 0)

    def per_source(g, carry):
        windows = []
        weight = weight_ref[g]
        for k in range(pairs):
            block = pool_ref[g, k * SUB : (k + 1) * SUB, :]
            for j in range(2):
                start = start_ref[(g * pairs + k) * 2 + j]
                select = jnp.where(steps == start, 1.0, 0.0).astype(jnp.bfloat16)
                parts = jnp.concatenate(
                    [block[:, (2 * j + p) * SUB : (2 * j + p + 1) * SUB] for p in range(2)], 0
                )
                windows.append(jnp.dot(parts, select, preferred_element_type=jnp.float32) * weight)
        for i, window in enumerate(windows):
            at = g * pairs * 2 + i
            row, lane_block = row_ref[at], block_ref[at]
            for p in range(2):
                for h in range(2):
                    acc[p, lane_block + h, pl.ds(row, SUB), :] += window[
                        p * SUB : (p + 1) * SUB, h * LANES : (h + 1) * LANES
                    ]
        return carry

    lax.fori_loop(0, pool_ref.shape[0], per_source, 0)

    group = min(16, rows_out)
    width = min(LANES, block_len)

    def per_group(i, carry):
        for h in range(block_len // width):
            values = []
            for a in range(tile_count):
                first = a * block_len + h * width
                lane = first % LANES
                rows = pl.ds(SUB + i * group, group)
                values.append(
                    tuple(acc[p, first // LANES, rows, lane : lane + width] for p in range(2))
                )
            lanes = slice(h * width, (h + 1) * width)
            for m, (re, im) in enumerate(fourier(values)):
                c, s = cos_ref[m : m + 1, lanes], sin_ref[m : m + 1, lanes]
                turned = (re * c - im * s, re * s + im * c)
                for p in range(2):
                    first = p * block_len + h * width
                    out_ref[m, pl.ds(i * group, group), first : first + width] = turned[p].astype(
                        jnp.bfloat16
                    )
        return carry

    lax.fori_loop(0, rows_out // group, per_group, 0)


def column_kernel(got_ref, second_ref, last_ref, out_ref, mid, mixed):
    tile_count, rows_here, wide = got_ref.shape
    block_len = wide // 2

    def second(t, carry):
        mid[t] = jnp.dot(got_ref[t], second_ref[...], preferred_element_type=jnp.float32)
        return carry

    lax.fori_loop(0, tile_count, second, 0)
    group = min(16, rows_here)
    width = min(LANES, block_len)

    def per_group(i, carry):
        rows = pl.ds(i * group, group)
        for h in range(block_len // width):
            values = [
                tuple(
                    mid[t, rows, p * block_len + h * width : p * block_len + (h + 1) * width]
                    for p in range(2)
                )
                for t in range(tile_count)
            ]
            for c, parts in enumerate(fourier(values)):
                for p in range(2):
                    mixed[
                        c,
                        pl.ds(p * rows_here + i * group, group),
                        h * width : (h + 1) * width,
                    ] = parts[p].astype(jnp.bfloat16)
        return carry

    lax.fori_loop(0, rows_here // group, per_group, 0)

    def last(c, carry):
        out_ref[c] = jnp.dot(
            last_ref[c], mixed[c], preferred_element_type=jnp.float32
        ).astype(jnp.bfloat16)
        return carry

    lax.fori_loop(0, tile_count, last, 0)


def turns(product, modulus):
    angles = (product % modulus) * (2.0 * math.pi / modulus)
    return np.cos(angles), np.sin(angles)


def make_tables(tile_count, epoch_count, block_len):
    grid_size = tile_count * block_len
    long_idx = np.arange(block_len)
    tile_idx = np.arange(tile_count)
    turn_cos, turn_sin = turns(tile_idx[:, None] * long_idx[None, :], grid_size)
    c, s = turns(long_idx[:, None] * long_idx[None, :], block_len)
    second = np.concatenate([np.concatenate([c, s], 1), np.concatenate([-s, c], 1)], 0)
    rows_here = block_len // epoch_count
    row = np.arange(block_len).reshape(epoch_count, 1, 1, rows_here)
    pixel = (long_idx[None, :] * tile_count + tile_idx[:, None])[None, :, :, None]
    c, s = turns(row * pixel, grid_size)
    last = np.concatenate([c, -s], -1)
    return (
        turn_cos.astype(np.float32),
        turn_sin.astype(np.float32),
        second.astype(jnp.bfloat16),
        last.astype(jnp.bfloat16),
    )


def vmem(count):
    return [pl.BlockSpec(memory_space=pltpu.VMEM)] * count


def smem(count):
    return [pl.BlockSpec(memory_space=pltpu.SMEM)] * count


def body(tables, owners, row_offsets, col_offsets, samples, coords, taper_rows, taper_cols):
    tile_count = lax.axis_size("tile")
    epoch_count = lax.axis_size("epoch")
    epoch_index = lax.axis_index("epoch")
    slot_owner = owners[0]
    n_slots = slot_owner.shape[0]
    pairs = (max(2, n_slots * 5 // (4 * tile_count)) + 1) // 2
    capacity = 2 * pairs
    info_rows = -(-capacity // 16) * 16
    block_rows = pairs * SUB + info_rows
    block_len = taper_cols.shape[0]
    rows_here = block_len // epoch_count
    params = pltpu.CompilerParams(vmem_limit_bytes=VMEM_BYTES)
    turn_cos, turn_sin, second, last = tables

    slot_idx = jnp.arange(n_slots, dtype=jnp.int32)
    same_before = (slot_owner[:, None] == slot_owner[None, :]) & (
        slot_idx[None, :] < slot_idx[:, None]
    )
    slot_rank = jnp.sum(same_before.astype(jnp.int32), 1)
    hit = (slot_owner[None, None, :] == jnp.arange(tile_count, dtype=jnp.int32)[:, None, None]) & (
        slot_rank[None, None, :] == jnp.arange(info_rows, dtype=jnp.int32)[None, :, None]
    )
    fields = [
        jnp.sum(jnp.where(hit, f, 0), 2)
        for f in (
            jnp.ones_like(slot_owner),
            row_offsets[0],
            col_offsets[0] // LANES,
            col_offsets[0] % LANES,
            slot_idx,
        )
    ]
    source = fields[4][:, :capacity].reshape(-1)
    info = jnp.pad(jnp.stack(fields[:4], -1), ((0, 0), (0, 0), (0, LANES - 4))).astype(jnp.bfloat16)
    data = jnp.concatenate([coords[0], samples[0].astype(jnp.float32)], 1)

    packed = pl.pallas_call(
        functools.partial(grid_kernel, pairs),
        out_shape=jax.ShapeDtypeStruct((tile_count, block_rows, LANES), jnp.bfloat16),
        in_specs=smem(1) + vmem(2),
        out_specs=vmem(1)[0],
        compiler_params=params,
        name="grid_slots",
    )(source, data, info)

    got = lax.all_to_all(packed, "tile", split_axis=0, concat_axis=0, tiled=True)
    pool = [got]
    for k in range(1, epoch_count):
        ring = [(e, (e + k) % epoch_count) for e in range(epoch_count)]
        pool.append(lax.ppermute(got, "epoch", ring))
    pool = jnp.concatenate(pool, 0) if epoch_count > 1 else got
    table = pool[:, pairs * SUB : pairs * SUB + capacity, :4].astype(jnp.int32)
    valid = table[:, :, 0] > 0
    counts = jnp.sum(valid.reshape(epoch_count, -1).astype(jnp.float32), 1)
    weight = jnp.repeat(1.0 / jnp.maximum(counts, 1.0), tile_count)
    first_row = table[:, :, 1] - epoch_index * rows_here + SUB
    inside = valid & (first_row > 0) & (first_row < rows_here + SUB)
    spare = rows_here + 2 * SUB
    place_row = jnp.where(inside, first_row, spare).reshape(-1)

    sent = pl.pallas_call(
        functools.partial(place_kernel, pairs, tile_count),
        out_shape=jax.ShapeDtypeStruct((tile_count, rows_here, 2 * block_len), jnp.bfloat16),
        in_specs=smem(4) + vmem(3),
        out_specs=vmem(1)[0],
        scratch_shapes=[
            pltpu.VMEM((2, tile_count * block_len // LANES + 1, spare + SUB, LANES), jnp.float32)
        ],
        compiler_params=params,
        name="place_subgrids",
    )(
        place_row,
        table[:, :, 2].reshape(-1),
        table[:, :, 3].reshape(-1),
        weight,
        pool,
        jnp.asarray(turn_cos),
        jnp.asarray(turn_sin),
    )

    gathered = lax.all_to_all(sent, "tile", split_axis=0, concat_axis=0, tiled=True)
    last_here = lax.dynamic_index_in_dim(jnp.asarray(last), epoch_index, 0, keepdims=False)
    partial_image = pl.pallas_call(
        column_kernel,
        out_shape=jax.ShapeDtypeStruct((tile_count, block_len, block_len), jnp.bfloat16),
        in_specs=vmem(3),
        out_specs=vmem(1)[0],
        scratch_shapes=[
            pltpu.VMEM((tile_count, rows_here, 2 * block_len), jnp.float32),
            pltpu.VMEM((tile_count, 2 * rows_here, block_len), jnp.bfloat16),
        ],
        compiler_params=params,
        name="column_sections",
    )(gathered, jnp.asarray(second), last_here)

    kept = tile_count // epoch_count

    def share(k):
        to = (epoch_index + k) % epoch_count
        return lax.dynamic_slice_in_dim(partial_image, to * kept, kept, 0)

    image_sum = share(0).astype(jnp.float32)
    for k in range(1, epoch_count):
        ring = [(e, (e + k) % epoch_count) for e in range(epoch_count)]
        image_sum = image_sum + lax.ppermute(share(k), "epoch", ring).astype(jnp.float32)
    image_scale = math.sqrt(n_slots) / (64.0 * tile_count * math.sqrt(epoch_count))
    return image_sum * (image_scale * taper_rows)[:, :, None] * taper_cols[None, None, :]


def solution(mesh):
    placed = (
        P("epoch", "tile"),
        P("epoch", "tile"),
        P("epoch", "tile"),
        P("epoch", "tile", None, None),
        P("epoch", "tile", None, None),
        P("epoch", None),
        P("tile"),
    )

    def whole(owners, row_offsets, col_offsets, samples, coords, taper_rows, taper_cols):
        tables = make_tables(
            mesh.shape["tile"], mesh.shape["epoch"], taper_cols.shape[0] // mesh.shape["tile"]
        )
        return jax.shard_map(
            functools.partial(body, tables),
            mesh=mesh,
            in_specs=placed,
            out_specs=P("epoch", None, "tile"),
            check_vma=False,
        )(owners, row_offsets, col_offsets, samples, coords, taper_rows, taper_cols)

    return whole
```

```python
import functools
import math

import jax
import jax.numpy as jnp
import numpy as np
from jax import lax
from jax.experimental import pallas as pl
from jax.experimental.pallas import tpu as pltpu
from jax.sharding import PartitionSpec as P

SUB = 32
LANES = 128
VMEM_BYTES = 56 * 1024 * 1024


def kernel_weights(distance):
    return jnp.square(jnp.maximum(1.0 - jnp.square(distance * 0.25), 0.0))


def fourier(values):
    count = len(values)
    if count == 1:
        return values
    if count == 2:
        (ar, ai), (br, bi) = values
        return [(ar + br, ai + bi), (ar - br, ai - bi)]
    even, odd = fourier(values[0::2]), fourier(values[1::2])
    low, high = [], []
    for k in range(count // 2):
        (er, ei), (orr, oi) = even[k], odd[k]
        if k == 0:
            tr, ti = orr, oi
        elif 4 * k == count:
            tr, ti = -oi, orr
        elif 8 * k == count:
            s = math.sqrt(0.5)
            tr, ti = (orr - oi) * s, (orr + oi) * s
        elif 8 * k == 3 * count:
            s = math.sqrt(0.5)
            tr, ti = (orr + oi) * -s, (orr - oi) * s
        else:
            c, s = math.cos(2 * math.pi * k / count), math.sin(2 * math.pi * k / count)
            tr, ti = orr * c - oi * s, orr * s + oi * c
        low.append((er + tr, ei + ti))
        high.append((er - tr, ei - ti))
    return low + high


def grid_kernel(pairs, src_ref, data_ref, info_ref, out_ref):
    cells = lax.broadcasted_iota(jnp.int32, (SUB, data_ref.shape[2]), 0).astype(jnp.float32)

    def one(slot):
        data = data_ref[slot]
        along_u = kernel_weights(cells - data[0:1]).astype(jnp.bfloat16)
        along_v = kernel_weights(cells - data[1:2])
        weighted = jnp.concatenate([data[2:3] * along_v, data[3:4] * along_v], 0)
        return lax.dot_general(
            along_u,
            weighted.astype(jnp.bfloat16),
            (((1,), (1,)), ((), ())),
            preferred_element_type=jnp.float32,
        )

    def per_tile(tile, carry):
        for k in range(pairs):
            at = (tile * pairs + k) * 2
            both = jnp.concatenate([one(src_ref[at]), one(src_ref[at + 1])], 1)
            out_ref[tile, k * SUB : (k + 1) * SUB, :] = both.astype(jnp.bfloat16)
        out_ref[tile, pairs * SUB :, :] = info_ref[tile]
        return carry

    lax.fori_loop(0, out_ref.shape[0], per_tile, 0)


def add_slots(pairs, row_ref, block_ref, start_ref, weight_ref, pool_ref, acc):
    lane_blocks, acc_rows = acc.shape[1], acc.shape[2]

    def clear(i, carry):
        acc[0, i] = jnp.zeros((acc_rows, LANES), jnp.float32)
        acc[1, i] = jnp.zeros((acc_rows, LANES), jnp.float32)
        return carry

    lax.fori_loop(0, lane_blocks, clear, 0)
    shape = (SUB, 2 * LANES)
    steps = lax.broadcasted_iota(jnp.int32, shape, 1) - lax.broadcasted_iota(jnp.int32, shape, 0)

    def per_source(g, carry):
        windows = []
        weight = weight_ref[g]
        for k in range(pairs):
            block = pool_ref[g, k * SUB : (k + 1) * SUB, :]
            for j in range(2):
                start = start_ref[(g * pairs + k) * 2 + j]
                select = jnp.where(steps == start, 1.0, 0.0).astype(jnp.bfloat16)
                parts = jnp.concatenate(
                    [block[:, (2 * j + p) * SUB : (2 * j + p + 1) * SUB] for p in range(2)], 0
                )
                windows.append(jnp.dot(parts, select, preferred_element_type=jnp.float32) * weight)
        for i, window in enumerate(windows):
            at = g * pairs * 2 + i
            row, lane_block = row_ref[at], block_ref[at]
            for p in range(2):
                for h in range(2):
                    acc[p, lane_block + h, pl.ds(row, SUB), :] += window[
                        p * SUB : (p + 1) * SUB, h * LANES : (h + 1) * LANES
                    ]
        return carry

    lax.fori_loop(0, pool_ref.shape[0], per_source, 0)


def place_kernel(pairs, row_ref, block_ref, start_ref, weight_ref, pool_ref, band_ref, acc):
    add_slots(pairs, row_ref, block_ref, start_ref, weight_ref, pool_ref, acc)
    rows_out = band_ref.shape[2]

    def put(i, carry):
        for p in range(2):
            band_ref[p, i] = acc[p, i, SUB : SUB + rows_out, :].astype(jnp.bfloat16)
        return carry

    lax.fori_loop(0, band_ref.shape[1], put, 0)


def rows_kernel(
    pairs,
    row_ref,
    block_ref,
    start_ref,
    weight_ref,
    pool_ref,
    band_ref,
    cos_ref,
    sin_ref,
    second_ref,
    *rest,
):
    out_refs, (acc, turned_ref) = rest[:-2], rest[-2:]
    add_slots(pairs, row_ref, block_ref, start_ref, weight_ref, pool_ref, acc)
    tile_count, rows_out, wide = turned_ref.shape
    block_len = wide // 2
    group = min(16, rows_out)
    width = min(LANES, block_len)

    def per_group(i, carry):
        for h in range(block_len // width):
            values = []
            for a in range(tile_count):
                first = a * block_len + h * width
                lane, at = first % LANES, first // LANES
                values.append(
                    tuple(
                        acc[p, at, pl.ds(SUB + i * group, group), lane : lane + width]
                        + band_ref[p, at, pl.ds(i * group, group), lane : lane + width].astype(
                            jnp.float32
                        )
                        for p in range(2)
                    )
                )
            lanes = slice(h * width, (h + 1) * width)
            for m, (re, im) in enumerate(fourier(values)):
                c, s = cos_ref[m : m + 1, lanes], sin_ref[m : m + 1, lanes]
                turned = (re * c - im * s, re * s + im * c)
                for p in range(2):
                    first = p * block_len + h * width
                    turned_ref[m, pl.ds(i * group, group), first : first + width] = turned[
                        p
                    ].astype(jnp.bfloat16)
        return carry

    lax.fori_loop(0, rows_out // group, per_group, 0)

    def per_tile(m, carry):
        moved = jnp.dot(turned_ref[m], second_ref[...], preferred_element_type=jnp.float32)
        for j, out_ref in enumerate(out_refs):
            out_ref[m] = moved[:, j * 2 * width : (j + 1) * 2 * width].astype(jnp.bfloat16)
        return carry

    lax.fori_loop(0, tile_count, per_tile, 0)


def column_kernel(epoch_ref, got_ref, last_ref, *rest):
    out_refs, mixed = rest[:-1], rest[-1]
    tile_count, rows_here, wide = got_ref.shape
    width = wide // 2
    group = min(16, rows_here)

    def per_group(i, carry):
        values = [
            tuple(
                got_ref[t, pl.ds(i * group, group), p * width : (p + 1) * width].astype(jnp.float32)
                for p in range(2)
            )
            for t in range(tile_count)
        ]
        for c, parts in enumerate(fourier(values)):
            for p in range(2):
                mixed[c, pl.ds(p * rows_here + i * group, group), :] = parts[p].astype(jnp.bfloat16)
        return carry

    lax.fori_loop(0, rows_here // group, per_group, 0)
    epoch_count = len(out_refs)
    kept = tile_count // epoch_count
    for k, out_ref in enumerate(out_refs):
        first = lax.rem(epoch_ref[0] + k, epoch_count) * kept

        def last(c, carry, out_ref=out_ref, first=first):
            out_ref[c] = jnp.dot(
                last_ref[first + c], mixed[first + c], preferred_element_type=jnp.float32
            ).astype(jnp.bfloat16)
            return carry

        lax.fori_loop(0, kept, last, 0)


def turns(product, modulus):
    angles = (product % modulus) * (2.0 * math.pi / modulus)
    return np.cos(angles), np.sin(angles)


def make_tables(tile_count, epoch_count, block_len):
    grid_size = tile_count * block_len
    long_idx = np.arange(block_len)
    tile_idx = np.arange(tile_count)
    turn_cos, turn_sin = turns(tile_idx[:, None] * long_idx[None, :], grid_size)
    c, s = turns(long_idx[:, None] * long_idx[None, :], block_len)
    second = np.stack([np.stack([c, s], 1), np.stack([-s, c], 1)], 0)
    width = min(LANES, block_len)
    second = second.reshape(2 * block_len, 2, block_len // width, width)
    second = second.transpose(0, 2, 1, 3).reshape(2 * block_len, 2 * block_len)
    rows_here = block_len // epoch_count
    row = np.arange(block_len).reshape(epoch_count, 1, 1, rows_here)
    pixel = (long_idx[None, :] * tile_count + tile_idx[:, None])[None, :, :, None]
    c, s = turns(row * pixel, grid_size)
    last = np.concatenate([c, -s], -1)
    return (
        turn_cos.astype(np.float32),
        turn_sin.astype(np.float32),
        second.astype(jnp.bfloat16),
        last.astype(jnp.bfloat16),
    )


def vmem(count):
    return [pl.BlockSpec(memory_space=pltpu.VMEM)] * count


def smem(count):
    return [pl.BlockSpec(memory_space=pltpu.SMEM)] * count


def body(tables, owners, row_offsets, col_offsets, samples, coords, taper_rows, taper_cols):
    tile_count = lax.axis_size("tile")
    epoch_count = lax.axis_size("epoch")
    epoch_index = lax.axis_index("epoch")
    slot_owner = owners[0]
    n_slots = slot_owner.shape[0]
    pairs = (max(2, n_slots * 5 // (4 * tile_count)) + 1) // 2
    capacity = 2 * pairs
    info_rows = -(-capacity // 16) * 16
    block_rows = pairs * SUB + info_rows
    block_len = taper_cols.shape[0]
    rows_here = block_len // epoch_count
    params = pltpu.CompilerParams(vmem_limit_bytes=VMEM_BYTES)
    turn_cos, turn_sin, second, last = tables

    slot_idx = jnp.arange(n_slots, dtype=jnp.int32)
    same_before = (slot_owner[:, None] == slot_owner[None, :]) & (
        slot_idx[None, :] < slot_idx[:, None]
    )
    slot_rank = jnp.sum(same_before.astype(jnp.int32), 1)
    hit = (slot_owner[None, None, :] == jnp.arange(tile_count, dtype=jnp.int32)[:, None, None]) & (
        slot_rank[None, None, :] == jnp.arange(info_rows, dtype=jnp.int32)[None, :, None]
    )
    fields = [
        jnp.sum(jnp.where(hit, f, 0), 2)
        for f in (
            jnp.ones_like(slot_owner),
            row_offsets[0],
            col_offsets[0] // LANES,
            col_offsets[0] % LANES,
            slot_idx,
        )
    ]
    source = fields[4][:, :capacity].reshape(-1)
    info = jnp.pad(jnp.stack(fields[:4], -1), ((0, 0), (0, 0), (0, LANES - 4))).astype(jnp.bfloat16)
    data = jnp.concatenate([coords[0], samples[0].astype(jnp.float32)], 1)

    packed = pl.pallas_call(
        functools.partial(grid_kernel, pairs),
        out_shape=jax.ShapeDtypeStruct((tile_count, block_rows, LANES), jnp.bfloat16),
        in_specs=smem(1) + vmem(2),
        out_specs=vmem(1)[0],
        compiler_params=params,
        name="grid_slots",
    )(source, data, info)

    got = lax.all_to_all(packed, "tile", split_axis=0, concat_axis=0, tiled=True)
    others = []
    for k in range(1, epoch_count):
        ring = [(e, (e + k) % epoch_count) for e in range(epoch_count)]
        others.append(lax.ppermute(got, "epoch", ring))
    others = jnp.concatenate(others, 0) if epoch_count > 2 else others[0]
    spare = rows_here + 2 * SUB
    lane_blocks = tile_count * block_len // LANES

    def places(pool):
        table = pool[:, pairs * SUB : pairs * SUB + capacity, :4].astype(jnp.int32)
        valid = table[:, :, 0] > 0
        counts = jnp.sum(table[:, :, 0].reshape(-1, tile_count * capacity), 1)
        weight = jnp.repeat(1.0 / jnp.maximum(counts, 1).astype(jnp.float32), tile_count)
        first_row = table[:, :, 1] - epoch_index * rows_here + SUB
        inside = valid & (first_row > 0) & (first_row < rows_here + SUB)
        place_row = jnp.where(inside, first_row, spare).reshape(-1)
        return place_row, table[:, :, 2].reshape(-1), table[:, :, 3].reshape(-1), weight, pool

    acc = pltpu.VMEM((2, lane_blocks + 1, spare + SUB, LANES), jnp.float32)
    band = pl.pallas_call(
        functools.partial(place_kernel, pairs),
        out_shape=jax.ShapeDtypeStruct((2, lane_blocks, rows_here, LANES), jnp.bfloat16),
        in_specs=smem(4) + vmem(1),
        out_specs=vmem(1)[0],
        scratch_shapes=[acc],
        compiler_params=params,
        cost_estimate=pl.CostEstimate(flops=8 * 10**9, bytes_accessed=10**7, transcendentals=0),
        name="place_subgrids",
    )(*places(got))

    width = min(LANES, block_len)
    chunks = block_len // width
    sent = pl.pallas_call(
        functools.partial(rows_kernel, pairs),
        out_shape=[
            jax.ShapeDtypeStruct((tile_count, rows_here, 2 * width), jnp.bfloat16)
            for _ in range(chunks)
        ],
        in_specs=smem(4) + vmem(5),
        out_specs=vmem(chunks),
        scratch_shapes=[acc, pltpu.VMEM((tile_count, rows_here, 2 * block_len), jnp.bfloat16)],
        compiler_params=params,
        name="row_sections",
    )(*places(others), band, jnp.asarray(turn_cos), jnp.asarray(turn_sin), jnp.asarray(second))

    last_here = lax.dynamic_index_in_dim(jnp.asarray(last), epoch_index, 0, keepdims=False)
    kept = tile_count // epoch_count
    sums = []
    for chunk in sent:
        gathered = lax.all_to_all(chunk, "tile", split_axis=0, concat_axis=0, tiled=True)
        shares = pl.pallas_call(
            column_kernel,
            out_shape=[
                jax.ShapeDtypeStruct((kept, block_len, width), jnp.bfloat16)
                for _ in range(epoch_count)
            ],
            in_specs=smem(1) + vmem(2),
            out_specs=vmem(epoch_count),
            scratch_shapes=[pltpu.VMEM((tile_count, 2 * rows_here, width), jnp.bfloat16)],
            compiler_params=params,
            cost_estimate=pl.CostEstimate(
                flops=6 * 10**9, bytes_accessed=10**7, transcendentals=0
            ),
            name="column_sections",
        )(epoch_index.astype(jnp.int32).reshape(1), gathered, last_here)
        chunk_sum = shares[0].astype(jnp.float32)
        for k in range(1, epoch_count):
            ring = [(e, (e + k) % epoch_count) for e in range(epoch_count)]
            chunk_sum = chunk_sum + lax.ppermute(shares[k], "epoch", ring).astype(jnp.float32)
        sums.append(chunk_sum)
    image_sum = jnp.concatenate(sums, 2)
    image_scale = math.sqrt(n_slots) / (64.0 * tile_count * math.sqrt(epoch_count))
    return image_sum * (image_scale * taper_rows)[:, :, None] * taper_cols[None, None, :]


def solution(mesh):
    placed = (
        P("epoch", "tile"),
        P("epoch", "tile"),
        P("epoch", "tile"),
        P("epoch", "tile", None, None),
        P("epoch", "tile", None, None),
        P("epoch", None),
        P("tile"),
    )

    def whole(owners, row_offsets, col_offsets, samples, coords, taper_rows, taper_cols):
        tables = make_tables(
            mesh.shape["tile"], mesh.shape["epoch"], taper_cols.shape[0] // mesh.shape["tile"]
        )
        return jax.shard_map(
            functools.partial(body, tables),
            mesh=mesh,
            in_specs=placed,
            out_specs=P("epoch", None, "tile"),
            check_vma=False,
        )(owners, row_offsets, col_offsets, samples, coords, taper_rows, taper_cols)

    return whole
```

```python
import functools
import math

import jax
import jax.numpy as jnp
import numpy as np
from jax import lax
from jax.experimental import pallas as pl
from jax.experimental.pallas import tpu as pltpu
from jax.sharding import PartitionSpec as P

SUB = 32
LANES = 128
VMEM_BYTES = 56 * 1024 * 1024


def kernel_weights(distance):
    return jnp.square(jnp.maximum(1.0 - jnp.square(distance * 0.25), 0.0))


def fourier(values):
    count = len(values)
    if count == 1:
        return values
    if count == 2:
        (ar, ai), (br, bi) = values
        return [(ar + br, ai + bi), (ar - br, ai - bi)]
    even, odd = fourier(values[0::2]), fourier(values[1::2])
    low, high = [], []
    for k in range(count // 2):
        (er, ei), (orr, oi) = even[k], odd[k]
        if k == 0:
            tr, ti = orr, oi
        elif 4 * k == count:
            tr, ti = -oi, orr
        elif 8 * k == count:
            s = math.sqrt(0.5)
            tr, ti = (orr - oi) * s, (orr + oi) * s
        elif 8 * k == 3 * count:
            s = math.sqrt(0.5)
            tr, ti = (orr + oi) * -s, (orr - oi) * s
        else:
            c, s = math.cos(2 * math.pi * k / count), math.sin(2 * math.pi * k / count)
            tr, ti = orr * c - oi * s, orr * s + oi * c
        low.append((er + tr, ei + ti))
        high.append((er - tr, ei - ti))
    return low + high


def grid_kernel(pairs, src_ref, data_ref, info_ref, out_ref):
    cells = lax.broadcasted_iota(jnp.int32, (SUB, data_ref.shape[2]), 0).astype(jnp.float32)

    def one(slot):
        data = data_ref[slot]
        along_u = kernel_weights(cells - data[0:1]).astype(jnp.bfloat16)
        along_v = kernel_weights(cells - data[1:2])
        weighted = jnp.concatenate([data[2:3] * along_v, data[3:4] * along_v], 0)
        return lax.dot_general(
            along_u,
            weighted.astype(jnp.bfloat16),
            (((1,), (1,)), ((), ())),
            preferred_element_type=jnp.float32,
        )

    def per_tile(tile, carry):
        for k in range(pairs):
            at = (tile * pairs + k) * 2
            both = jnp.concatenate([one(src_ref[at]), one(src_ref[at + 1])], 1)
            out_ref[tile, k * SUB : (k + 1) * SUB, :] = both.astype(jnp.bfloat16)
        out_ref[tile, pairs * SUB :, :] = info_ref[tile]
        return carry

    lax.fori_loop(0, out_ref.shape[0], per_tile, 0)


def add_slots(pairs, row_ref, block_ref, start_ref, weight_ref, pool_ref, acc):
    lane_blocks, acc_rows = acc.shape[1], acc.shape[2]

    def clear(i, carry):
        acc[0, i] = jnp.zeros((acc_rows, LANES), jnp.float32)
        acc[1, i] = jnp.zeros((acc_rows, LANES), jnp.float32)
        return carry

    lax.fori_loop(0, lane_blocks, clear, 0)
    shape = (SUB, 2 * LANES)
    steps = lax.broadcasted_iota(jnp.int32, shape, 1) - lax.broadcasted_iota(jnp.int32, shape, 0)

    def per_source(g, carry):
        windows = []
        weight = weight_ref[g]
        for k in range(pairs):
            block = pool_ref[g, k * SUB : (k + 1) * SUB, :]
            for j in range(2):
                start = start_ref[(g * pairs + k) * 2 + j]
                select = jnp.where(steps == start, 1.0, 0.0).astype(jnp.bfloat16)
                parts = jnp.concatenate(
                    [block[:, (2 * j + p) * SUB : (2 * j + p + 1) * SUB] for p in range(2)], 0
                )
                windows.append(jnp.dot(parts, select, preferred_element_type=jnp.float32) * weight)
        for i, window in enumerate(windows):
            at = g * pairs * 2 + i
            row, lane_block = row_ref[at], block_ref[at]
            for p in range(2):
                for h in range(2):
                    acc[p, lane_block + h, pl.ds(row, SUB), :] += window[
                        p * SUB : (p + 1) * SUB, h * LANES : (h + 1) * LANES
                    ]
        return carry

    lax.fori_loop(0, pool_ref.shape[0], per_source, 0)


def place_kernel(pairs, row_ref, block_ref, start_ref, weight_ref, pool_ref, band_ref, acc):
    add_slots(pairs, row_ref, block_ref, start_ref, weight_ref, pool_ref, acc)
    rows_out = band_ref.shape[2]

    def put(i, carry):
        for p in range(2):
            band_ref[p, i] = acc[p, i, SUB : SUB + rows_out, :].astype(jnp.bfloat16)
        return carry

    lax.fori_loop(0, band_ref.shape[1], put, 0)


def rows_kernel(
    pairs,
    row_ref,
    block_ref,
    start_ref,
    weight_ref,
    pool_ref,
    band_ref,
    cos_ref,
    sin_ref,
    second_ref,
    *rest,
):
    out_refs, (acc, turned_ref) = rest[:-2], rest[-2:]
    add_slots(pairs, row_ref, block_ref, start_ref, weight_ref, pool_ref, acc)
    tile_count, rows_out, wide = turned_ref.shape
    block_len = wide // 2
    group = min(16, rows_out)
    width = min(LANES, block_len)

    def per_group(i, carry):
        for h in range(block_len // width):
            values = []
            for a in range(tile_count):
                first = a * block_len + h * width
                lane, at = first % LANES, first // LANES
                values.append(
                    tuple(
                        acc[p, at, pl.ds(SUB + i * group, group), lane : lane + width]
                        + band_ref[p, at, pl.ds(i * group, group), lane : lane + width].astype(
                            jnp.float32
                        )
                        for p in range(2)
                    )
                )
            lanes = slice(h * width, (h + 1) * width)
            for m, (re, im) in enumerate(fourier(values)):
                c, s = cos_ref[m : m + 1, lanes], sin_ref[m : m + 1, lanes]
                turned = (re * c - im * s, re * s + im * c)
                for p in range(2):
                    first = p * block_len + h * width
                    turned_ref[m, pl.ds(i * group, group), first : first + width] = turned[
                        p
                    ].astype(jnp.bfloat16)
        return carry

    lax.fori_loop(0, rows_out // group, per_group, 0)

    def per_tile(m, carry):
        moved = jnp.dot(turned_ref[m], second_ref[...], preferred_element_type=jnp.float32)
        for j, out_ref in enumerate(out_refs):
            out_ref[m] = moved[:, j * 2 * width : (j + 1) * 2 * width].astype(jnp.bfloat16)
        return carry

    lax.fori_loop(0, tile_count, per_tile, 0)


def columns_kernel(tile_count, epoch_count, chunks, *refs):
    sent, last_ref, outs = refs[:chunks], refs[chunks], refs[chunks + 1 : 2 * chunks + 1]
    got, mixed, share, landed, t_send, t_recv, x_send, x_recv, own_sem = refs[2 * chunks + 1 :]
    rows_here, width = got.shape[2], got.shape[3] // 2
    kept = tile_count // epoch_count
    me, epoch = lax.axis_index("tile"), lax.axis_index("epoch")
    mesh_id = pl.DeviceIdType.MESH

    barrier = pltpu.get_barrier_semaphore()

    def greet(k, carry):
        peer = lax.rem(me + k, tile_count)
        pl.semaphore_signal(barrier, inc=1, device_id={"tile": peer}, device_id_type=mesh_id)
        return carry

    lax.fori_loop(1, tile_count, greet, 0)
    for k in range(1, epoch_count):
        peer = lax.rem(epoch + k, epoch_count)
        pl.semaphore_signal(barrier, inc=1, device_id={"epoch": peer}, device_id_type=mesh_id)
    pl.semaphore_wait(barrier, tile_count + epoch_count - 2)

    def tile_copy(j, k):
        peer = lax.rem(me + k, tile_count)
        return pltpu.make_async_remote_copy(
            src_ref=sent[j].at[peer],
            dst_ref=got.at[j, me],
            send_sem=t_send.at[j * tile_count + k],
            recv_sem=t_recv.at[j * tile_count + k],
            device_id={"tile": peer},
            device_id_type=mesh_id,
        )

    def epoch_copy(j, k, c):
        at = (j * (epoch_count - 1) + k - 1) * kept + c
        return pltpu.make_async_remote_copy(
            src_ref=share.at[j, k - 1, c],
            dst_ref=landed.at[j, k - 1, c],
            send_sem=x_send.at[at],
            recv_sem=x_recv.at[at],
            device_id={"epoch": lax.rem(epoch + k, epoch_count)},
            device_id_type=mesh_id,
        )

    def own_copy(j):
        return pltpu.make_async_copy(sent[j].at[me], got.at[j, me], own_sem.at[j])

    for j in range(chunks):

        def send(k, carry, j=j):
            tile_copy(j, k).start()
            return carry

        lax.fori_loop(1, tile_count, send, 0)
        own_copy(j).start()

    group = min(16, rows_here)
    for j in range(chunks):

        def receive(k, carry, j=j):
            tile_copy(j, k).wait_recv()
            return carry

        lax.fori_loop(1, tile_count, receive, 0)
        own_copy(j).wait()

        def per_group(i, carry, j=j):
            values = [
                tuple(
                    got[
                        j, t, pl.ds(i * group, group), p * width : (p + 1) * width
                    ].astype(jnp.float32)
                    for p in range(2)
                )
                for t in range(tile_count)
            ]
            for c, parts in enumerate(fourier(values)):
                for p in range(2):
                    mixed[c, pl.ds(p * rows_here + i * group, group), :] = parts[p].astype(
                        jnp.bfloat16
                    )
            return carry

        lax.fori_loop(0, rows_here // group, per_group, 0)

        for k in range(1, epoch_count):
            first = lax.rem(epoch + k, epoch_count) * kept

            def away(c, carry, j=j, k=k, first=first):
                share[j, k - 1, c] = jnp.dot(
                    last_ref[first + c], mixed[first + c], preferred_element_type=jnp.float32
                ).astype(jnp.bfloat16)
                epoch_copy(j, k, c).start()
                return carry

            lax.fori_loop(0, kept, away, 0)

        def home(c, carry, j=j):
            outs[j][c] = jnp.dot(
                last_ref[epoch * kept + c],
                mixed[epoch * kept + c],
                preferred_element_type=jnp.float32,
            )
            return carry

        lax.fori_loop(0, kept, home, 0)

    for j in range(chunks):

        def sent_all(k, carry, j=j):
            tile_copy(j, k).wait_send()
            return carry

        lax.fori_loop(1, tile_count, sent_all, 0)
        for k in range(1, epoch_count):

            def add(c, carry, j=j, k=k):
                epoch_copy(j, k, c).wait()
                outs[j][c] += landed[j, k - 1, c].astype(jnp.float32)
                return carry

            lax.fori_loop(0, kept, add, 0)


def turns(product, modulus):
    angles = (product % modulus) * (2.0 * math.pi / modulus)
    return np.cos(angles), np.sin(angles)


def make_tables(tile_count, epoch_count, block_len):
    grid_size = tile_count * block_len
    long_idx = np.arange(block_len)
    tile_idx = np.arange(tile_count)
    turn_cos, turn_sin = turns(tile_idx[:, None] * long_idx[None, :], grid_size)
    c, s = turns(long_idx[:, None] * long_idx[None, :], block_len)
    second = np.stack([np.stack([c, s], 1), np.stack([-s, c], 1)], 0)
    width = min(LANES, block_len)
    second = second.reshape(2 * block_len, 2, block_len // width, width)
    second = second.transpose(0, 2, 1, 3).reshape(2 * block_len, 2 * block_len)
    rows_here = block_len // epoch_count
    row = np.arange(block_len).reshape(epoch_count, 1, 1, rows_here)
    pixel = (long_idx[None, :] * tile_count + tile_idx[:, None])[None, :, :, None]
    c, s = turns(row * pixel, grid_size)
    last = np.concatenate([c, -s], -1)
    return (
        turn_cos.astype(np.float32),
        turn_sin.astype(np.float32),
        second.astype(jnp.bfloat16),
        last.astype(jnp.bfloat16),
    )


def vmem(count):
    return [pl.BlockSpec(memory_space=pltpu.VMEM)] * count


def smem(count):
    return [pl.BlockSpec(memory_space=pltpu.SMEM)] * count


def body(tables, owners, row_offsets, col_offsets, samples, coords, taper_rows, taper_cols):
    tile_count = lax.axis_size("tile")
    epoch_count = lax.axis_size("epoch")
    epoch_index = lax.axis_index("epoch")
    slot_owner = owners[0]
    n_slots = slot_owner.shape[0]
    pairs = (max(2, n_slots * 5 // (4 * tile_count)) + 1) // 2
    capacity = 2 * pairs
    info_rows = -(-capacity // 16) * 16
    block_rows = pairs * SUB + info_rows
    block_len = taper_cols.shape[0]
    rows_here = block_len // epoch_count
    params = pltpu.CompilerParams(vmem_limit_bytes=VMEM_BYTES)
    turn_cos, turn_sin, second, last = tables

    slot_idx = jnp.arange(n_slots, dtype=jnp.int32)
    same_before = (slot_owner[:, None] == slot_owner[None, :]) & (
        slot_idx[None, :] < slot_idx[:, None]
    )
    slot_rank = jnp.sum(same_before.astype(jnp.int32), 1)
    hit = (slot_owner[None, None, :] == jnp.arange(tile_count, dtype=jnp.int32)[:, None, None]) & (
        slot_rank[None, None, :] == jnp.arange(info_rows, dtype=jnp.int32)[None, :, None]
    )
    fields = [
        jnp.sum(jnp.where(hit, f, 0), 2)
        for f in (
            jnp.ones_like(slot_owner),
            row_offsets[0],
            col_offsets[0] // LANES,
            col_offsets[0] % LANES,
            slot_idx,
        )
    ]
    source = fields[4][:, :capacity].reshape(-1)
    info = jnp.pad(jnp.stack(fields[:4], -1), ((0, 0), (0, 0), (0, LANES - 4))).astype(jnp.bfloat16)
    data = jnp.concatenate([coords[0], samples[0].astype(jnp.float32)], 1)

    packed = pl.pallas_call(
        functools.partial(grid_kernel, pairs),
        out_shape=jax.ShapeDtypeStruct((tile_count, block_rows, LANES), jnp.bfloat16),
        in_specs=smem(1) + vmem(2),
        out_specs=vmem(1)[0],
        compiler_params=params,
        name="grid_slots",
    )(source, data, info)

    got = lax.all_to_all(packed, "tile", split_axis=0, concat_axis=0, tiled=True)
    others = []
    for k in range(1, epoch_count):
        ring = [(e, (e + k) % epoch_count) for e in range(epoch_count)]
        others.append(lax.ppermute(got, "epoch", ring))
    others = jnp.concatenate(others, 0) if epoch_count > 2 else others[0]
    spare = rows_here + 2 * SUB
    lane_blocks = tile_count * block_len // LANES

    def places(pool):
        table = pool[:, pairs * SUB : pairs * SUB + capacity, :4].astype(jnp.int32)
        valid = table[:, :, 0] > 0
        counts = jnp.sum(table[:, :, 0].reshape(-1, tile_count * capacity), 1)
        weight = jnp.repeat(1.0 / jnp.maximum(counts, 1).astype(jnp.float32), tile_count)
        first_row = table[:, :, 1] - epoch_index * rows_here + SUB
        inside = valid & (first_row > 0) & (first_row < rows_here + SUB)
        place_row = jnp.where(inside, first_row, spare).reshape(-1)
        return place_row, table[:, :, 2].reshape(-1), table[:, :, 3].reshape(-1), weight, pool

    acc = pltpu.VMEM((2, lane_blocks + 1, spare + SUB, LANES), jnp.float32)
    band = pl.pallas_call(
        functools.partial(place_kernel, pairs),
        out_shape=jax.ShapeDtypeStruct((2, lane_blocks, rows_here, LANES), jnp.bfloat16),
        in_specs=smem(4) + vmem(1),
        out_specs=vmem(1)[0],
        scratch_shapes=[acc],
        compiler_params=params,
        cost_estimate=pl.CostEstimate(flops=8 * 10**9, bytes_accessed=10**7, transcendentals=0),
        name="place_subgrids",
    )(*places(got))

    width = min(LANES, block_len)
    chunks = block_len // width
    sent = pl.pallas_call(
        functools.partial(rows_kernel, pairs),
        out_shape=[
            jax.ShapeDtypeStruct((tile_count, rows_here, 2 * width), jnp.bfloat16)
            for _ in range(chunks)
        ],
        in_specs=smem(4) + vmem(5),
        out_specs=vmem(chunks),
        scratch_shapes=[acc, pltpu.VMEM((tile_count, rows_here, 2 * block_len), jnp.bfloat16)],
        compiler_params=params,
        name="row_sections",
    )(*places(others), band, jnp.asarray(turn_cos), jnp.asarray(turn_sin), jnp.asarray(second))

    last_here = lax.dynamic_index_in_dim(jnp.asarray(last), epoch_index, 0, keepdims=False)
    kept = tile_count // epoch_count
    shares_shape = (chunks, epoch_count - 1, kept, block_len, width)
    tile_sems = pltpu.SemaphoreType.DMA((chunks * tile_count,))
    epoch_sems = pltpu.SemaphoreType.DMA((chunks * (epoch_count - 1) * kept,))
    sums = pl.pallas_call(
        functools.partial(columns_kernel, tile_count, epoch_count, chunks),
        out_shape=[
            jax.ShapeDtypeStruct((kept, block_len, width), jnp.float32) for _ in range(chunks)
        ],
        in_specs=vmem(chunks + 1),
        out_specs=vmem(chunks),
        scratch_shapes=[
            pltpu.VMEM((chunks, tile_count, rows_here, 2 * width), jnp.bfloat16),
            pltpu.VMEM((tile_count, 2 * rows_here, width), jnp.bfloat16),
            pltpu.VMEM(shares_shape, jnp.bfloat16),
            pltpu.VMEM(shares_shape, jnp.bfloat16),
            tile_sems,
            tile_sems,
            epoch_sems,
            epoch_sems,
            pltpu.SemaphoreType.DMA((chunks,)),
        ],
        compiler_params=pltpu.CompilerParams(
            vmem_limit_bytes=VMEM_BYTES, collective_id=0, has_side_effects=True
        ),
        name="columns",
    )(*sent, last_here)
    image_sum = jnp.concatenate(sums, 2)
    image_scale = math.sqrt(n_slots) / (64.0 * tile_count * math.sqrt(epoch_count))
    return image_sum * (image_scale * taper_rows)[:, :, None] * taper_cols[None, None, :]


def solution(mesh):
    placed = (
        P("epoch", "tile"),
        P("epoch", "tile"),
        P("epoch", "tile"),
        P("epoch", "tile", None, None),
        P("epoch", "tile", None, None),
        P("epoch", None),
        P("tile"),
    )

    def whole(owners, row_offsets, col_offsets, samples, coords, taper_rows, taper_cols):
        tables = make_tables(
            mesh.shape["tile"], mesh.shape["epoch"], taper_cols.shape[0] // mesh.shape["tile"]
        )
        return jax.shard_map(
            functools.partial(body, tables),
            mesh=mesh,
            in_specs=placed,
            out_specs=P("epoch", None, "tile"),
            check_vma=False,
        )(owners, row_offsets, col_offsets, samples, coords, taper_rows, taper_cols)

    return whole
```

```python
import functools
import math

import jax
import jax.numpy as jnp
import numpy as np
from jax import lax
from jax.experimental import pallas as pl
from jax.experimental.pallas import tpu as pltpu
from jax.sharding import PartitionSpec as P

SUB = 32
LANES = 128
VMEM_BYTES = 56 * 1024 * 1024


def kernel_weights(distance):
    return jnp.square(jnp.maximum(1.0 - jnp.square(distance * 0.25), 0.0))


def fourier(values):
    count = len(values)
    if count == 1:
        return values
    if count == 2:
        (ar, ai), (br, bi) = values
        return [(ar + br, ai + bi), (ar - br, ai - bi)]
    even, odd = fourier(values[0::2]), fourier(values[1::2])
    low, high = [], []
    for k in range(count // 2):
        (er, ei), (orr, oi) = even[k], odd[k]
        if k == 0:
            tr, ti = orr, oi
        elif 4 * k == count:
            tr, ti = -oi, orr
        elif 8 * k == count:
            s = math.sqrt(0.5)
            tr, ti = (orr - oi) * s, (orr + oi) * s
        elif 8 * k == 3 * count:
            s = math.sqrt(0.5)
            tr, ti = (orr + oi) * -s, (orr - oi) * s
        else:
            c, s = math.cos(2 * math.pi * k / count), math.sin(2 * math.pi * k / count)
            tr, ti = orr * c - oi * s, orr * s + oi * c
        low.append((er + tr, ei + ti))
        high.append((er - tr, ei - ti))
    return low + high


def grid_kernel(
    pairs, tile_count, epoch_count, src_ref, data_ref, info_ref, got_ref, others_ref, *scratch
):
    packed, t_send, t_recv, x_send, x_recv = scratch
    me, epoch = lax.axis_index("tile"), lax.axis_index("epoch")
    mesh_id = pl.DeviceIdType.MESH
    cells = lax.broadcasted_iota(jnp.int32, (SUB, data_ref.shape[2]), 0).astype(jnp.float32)

    barrier = pltpu.get_barrier_semaphore()

    def greet(k, carry):
        peer = lax.rem(me + k, tile_count)
        pl.semaphore_signal(barrier, inc=1, device_id={"tile": peer}, device_id_type=mesh_id)
        return carry

    lax.fori_loop(1, tile_count, greet, 0)
    for k in range(1, epoch_count):
        peer = lax.rem(epoch + k, epoch_count)
        pl.semaphore_signal(barrier, inc=1, device_id={"epoch": peer}, device_id_type=mesh_id)
    pl.semaphore_wait(barrier, tile_count + epoch_count - 2)

    def one(slot):
        data = data_ref[slot]
        along_u = kernel_weights(cells - data[0:1]).astype(jnp.bfloat16)
        along_v = kernel_weights(cells - data[1:2])
        weighted = jnp.concatenate([data[2:3] * along_v, data[3:4] * along_v], 0)
        return lax.dot_general(
            along_u,
            weighted.astype(jnp.bfloat16),
            (((1,), (1,)), ((), ())),
            preferred_element_type=jnp.float32,
        )

    def make(tile, out_ref):
        for k in range(pairs):
            at = (tile * pairs + k) * 2
            both = jnp.concatenate([one(src_ref[at]), one(src_ref[at + 1])], 1)
            out_ref[tile, k * SUB : (k + 1) * SUB, :] = both.astype(jnp.bfloat16)
        out_ref[tile, pairs * SUB :, :] = info_ref[tile]

    def tile_copy(k):
        peer = lax.rem(me + k, tile_count)
        return pltpu.make_async_remote_copy(
            src_ref=packed.at[peer],
            dst_ref=got_ref.at[me],
            send_sem=t_send.at[k],
            recv_sem=t_recv.at[k],
            device_id={"tile": peer},
            device_id_type=mesh_id,
        )

    def epoch_copy(k, j):
        origin = lax.rem(me + tile_count - k, tile_count)
        return pltpu.make_async_remote_copy(
            src_ref=got_ref.at[origin],
            dst_ref=others_ref.at[(j - 1) * tile_count + origin],
            send_sem=x_send.at[(j - 1) * tile_count + k],
            recv_sem=x_recv.at[(j - 1) * tile_count + k],
            device_id={"epoch": lax.rem(epoch + j, epoch_count)},
            device_id_type=mesh_id,
        )

    def send(k, carry):
        make(lax.rem(me + k, tile_count), packed)
        tile_copy(k).start()
        return carry

    make(me, got_ref)
    for j in range(1, epoch_count):
        epoch_copy(0, j).start()
    lax.fori_loop(1, tile_count, send, 0)

    def forward(k, carry):
        tile_copy(k).wait_recv()
        for j in range(1, epoch_count):
            epoch_copy(k, j).start()
        return carry

    lax.fori_loop(1, tile_count, forward, 0)

    def sent_all(k, carry):
        tile_copy(k).wait_send()
        return carry

    lax.fori_loop(1, tile_count, sent_all, 0)

    def crossed(k, carry):
        for j in range(1, epoch_count):
            epoch_copy(k, j).wait()
        return carry

    lax.fori_loop(0, tile_count, crossed, 0)


def add_slots(pairs, row_ref, block_ref, start_ref, weight_ref, pool_ref, acc):
    lane_blocks, acc_rows = acc.shape[1], acc.shape[2]

    def clear(i, carry):
        acc[0, i] = jnp.zeros((acc_rows, LANES), jnp.float32)
        acc[1, i] = jnp.zeros((acc_rows, LANES), jnp.float32)
        return carry

    lax.fori_loop(0, lane_blocks, clear, 0)
    shape = (SUB, 2 * LANES)
    steps = lax.broadcasted_iota(jnp.int32, shape, 1) - lax.broadcasted_iota(jnp.int32, shape, 0)

    def per_source(g, carry):
        windows = []
        weight = weight_ref[g]
        for k in range(pairs):
            block = pool_ref[g, k * SUB : (k + 1) * SUB, :]
            for j in range(2):
                start = start_ref[(g * pairs + k) * 2 + j]
                select = jnp.where(steps == start, 1.0, 0.0).astype(jnp.bfloat16)
                parts = jnp.concatenate(
                    [block[:, (2 * j + p) * SUB : (2 * j + p + 1) * SUB] for p in range(2)], 0
                )
                windows.append(jnp.dot(parts, select, preferred_element_type=jnp.float32) * weight)
        for i, window in enumerate(windows):
            at = g * pairs * 2 + i
            row, lane_block = row_ref[at], block_ref[at]
            for p in range(2):
                for h in range(2):
                    acc[p, lane_block + h, pl.ds(row, SUB), :] += window[
                        p * SUB : (p + 1) * SUB, h * LANES : (h + 1) * LANES
                    ]
        return carry

    lax.fori_loop(0, pool_ref.shape[0], per_source, 0)


def place_kernel(pairs, row_ref, block_ref, start_ref, weight_ref, pool_ref, band_ref, acc):
    add_slots(pairs, row_ref, block_ref, start_ref, weight_ref, pool_ref, acc)
    rows_out = band_ref.shape[2]

    def put(i, carry):
        for p in range(2):
            band_ref[p, i] = acc[p, i, SUB : SUB + rows_out, :].astype(jnp.bfloat16)
        return carry

    lax.fori_loop(0, band_ref.shape[1], put, 0)


def rows_kernel(
    pairs,
    row_ref,
    block_ref,
    start_ref,
    weight_ref,
    pool_ref,
    band_ref,
    cos_ref,
    sin_ref,
    second_ref,
    *rest,
):
    out_refs, (acc, turned_ref) = rest[:-2], rest[-2:]
    add_slots(pairs, row_ref, block_ref, start_ref, weight_ref, pool_ref, acc)
    tile_count, rows_out, wide = turned_ref.shape
    block_len = wide // 2
    group = min(16, rows_out)
    width = min(LANES, block_len)

    def per_group(i, carry):
        for h in range(block_len // width):
            values = []
            for a in range(tile_count):
                first = a * block_len + h * width
                lane, at = first % LANES, first // LANES
                values.append(
                    tuple(
                        acc[p, at, pl.ds(SUB + i * group, group), lane : lane + width]
                        + band_ref[p, at, pl.ds(i * group, group), lane : lane + width].astype(
                            jnp.float32
                        )
                        for p in range(2)
                    )
                )
            lanes = slice(h * width, (h + 1) * width)
            for m, (re, im) in enumerate(fourier(values)):
                c, s = cos_ref[m : m + 1, lanes], sin_ref[m : m + 1, lanes]
                turned = (re * c - im * s, re * s + im * c)
                for p in range(2):
                    first = p * block_len + h * width
                    turned_ref[m, pl.ds(i * group, group), first : first + width] = turned[
                        p
                    ].astype(jnp.bfloat16)
        return carry

    lax.fori_loop(0, rows_out // group, per_group, 0)

    def per_tile(m, carry):
        moved = jnp.dot(turned_ref[m], second_ref[...], preferred_element_type=jnp.float32)
        for j, out_ref in enumerate(out_refs):
            out_ref[m] = moved[:, j * 2 * width : (j + 1) * 2 * width].astype(jnp.bfloat16)
        return carry

    lax.fori_loop(0, tile_count, per_tile, 0)


def columns_kernel(tile_count, epoch_count, chunks, *refs):
    sent, last_ref, outs = refs[:chunks], refs[chunks], refs[chunks + 1 : 2 * chunks + 1]
    got, mixed, share, landed, t_send, t_recv, x_send, x_recv, own_sem = refs[2 * chunks + 1 :]
    rows_here, width = got.shape[2], got.shape[3] // 2
    kept = tile_count // epoch_count
    me, epoch = lax.axis_index("tile"), lax.axis_index("epoch")
    mesh_id = pl.DeviceIdType.MESH

    barrier = pltpu.get_barrier_semaphore()

    def greet(k, carry):
        peer = lax.rem(me + k, tile_count)
        pl.semaphore_signal(barrier, inc=1, device_id={"tile": peer}, device_id_type=mesh_id)
        return carry

    lax.fori_loop(1, tile_count, greet, 0)
    for k in range(1, epoch_count):
        peer = lax.rem(epoch + k, epoch_count)
        pl.semaphore_signal(barrier, inc=1, device_id={"epoch": peer}, device_id_type=mesh_id)
    pl.semaphore_wait(barrier, tile_count + epoch_count - 2)

    def tile_copy(j, k):
        peer = lax.rem(me + k, tile_count)
        return pltpu.make_async_remote_copy(
            src_ref=sent[j].at[peer],
            dst_ref=got.at[j, me],
            send_sem=t_send.at[j * tile_count + k],
            recv_sem=t_recv.at[j * tile_count + k],
            device_id={"tile": peer},
            device_id_type=mesh_id,
        )

    def epoch_copy(j, k, c):
        at = (j * (epoch_count - 1) + k - 1) * kept + c
        return pltpu.make_async_remote_copy(
            src_ref=share.at[j, k - 1, c],
            dst_ref=landed.at[j, k - 1, c],
            send_sem=x_send.at[at],
            recv_sem=x_recv.at[at],
            device_id={"epoch": lax.rem(epoch + k, epoch_count)},
            device_id_type=mesh_id,
        )

    def own_copy(j):
        return pltpu.make_async_copy(sent[j].at[me], got.at[j, me], own_sem.at[j])

    for j in range(chunks):

        def send(k, carry, j=j):
            tile_copy(j, k).start()
            return carry

        lax.fori_loop(1, tile_count, send, 0)
        own_copy(j).start()

    group = min(16, rows_here)
    for j in range(chunks):

        def receive(k, carry, j=j):
            tile_copy(j, k).wait_recv()
            return carry

        lax.fori_loop(1, tile_count, receive, 0)
        own_copy(j).wait()

        def per_group(i, carry, j=j):
            values = [
                tuple(
                    got[
                        j, t, pl.ds(i * group, group), p * width : (p + 1) * width
                    ].astype(jnp.float32)
                    for p in range(2)
                )
                for t in range(tile_count)
            ]
            for c, parts in enumerate(fourier(values)):
                for p in range(2):
                    mixed[c, pl.ds(p * rows_here + i * group, group), :] = parts[p].astype(
                        jnp.bfloat16
                    )
            return carry

        lax.fori_loop(0, rows_here // group, per_group, 0)

        for k in range(1, epoch_count):
            first = lax.rem(epoch + k, epoch_count) * kept

            def away(c, carry, j=j, k=k, first=first):
                share[j, k - 1, c] = jnp.dot(
                    last_ref[first + c], mixed[first + c], preferred_element_type=jnp.float32
                ).astype(jnp.bfloat16)
                epoch_copy(j, k, c).start()
                return carry

            lax.fori_loop(0, kept, away, 0)

        def home(c, carry, j=j):
            outs[j][c] = jnp.dot(
                last_ref[epoch * kept + c],
                mixed[epoch * kept + c],
                preferred_element_type=jnp.float32,
            )
            return carry

        lax.fori_loop(0, kept, home, 0)

    for j in range(chunks):

        def sent_all(k, carry, j=j):
            tile_copy(j, k).wait_send()
            return carry

        lax.fori_loop(1, tile_count, sent_all, 0)
        for k in range(1, epoch_count):

            def add(c, carry, j=j, k=k):
                epoch_copy(j, k, c).wait()
                outs[j][c] += landed[j, k - 1, c].astype(jnp.float32)
                return carry

            lax.fori_loop(0, kept, add, 0)


def turns(product, modulus):
    angles = (product % modulus) * (2.0 * math.pi / modulus)
    return np.cos(angles), np.sin(angles)


def make_tables(tile_count, epoch_count, block_len):
    grid_size = tile_count * block_len
    long_idx = np.arange(block_len)
    tile_idx = np.arange(tile_count)
    turn_cos, turn_sin = turns(tile_idx[:, None] * long_idx[None, :], grid_size)
    c, s = turns(long_idx[:, None] * long_idx[None, :], block_len)
    second = np.stack([np.stack([c, s], 1), np.stack([-s, c], 1)], 0)
    width = min(LANES, block_len)
    second = second.reshape(2 * block_len, 2, block_len // width, width)
    second = second.transpose(0, 2, 1, 3).reshape(2 * block_len, 2 * block_len)
    rows_here = block_len // epoch_count
    row = np.arange(block_len).reshape(epoch_count, 1, 1, rows_here)
    pixel = (long_idx[None, :] * tile_count + tile_idx[:, None])[None, :, :, None]
    c, s = turns(row * pixel, grid_size)
    last = np.concatenate([c, -s], -1)
    return (
        turn_cos.astype(np.float32),
        turn_sin.astype(np.float32),
        second.astype(jnp.bfloat16),
        last.astype(jnp.bfloat16),
    )


def vmem(count):
    return [pl.BlockSpec(memory_space=pltpu.VMEM)] * count


def smem(count):
    return [pl.BlockSpec(memory_space=pltpu.SMEM)] * count


def body(tables, owners, row_offsets, col_offsets, samples, coords, taper_rows, taper_cols):
    tile_count = lax.axis_size("tile")
    epoch_count = lax.axis_size("epoch")
    epoch_index = lax.axis_index("epoch")
    slot_owner = owners[0]
    n_slots = slot_owner.shape[0]
    pairs = (max(2, n_slots * 5 // (4 * tile_count)) + 1) // 2
    capacity = 2 * pairs
    info_rows = -(-capacity // 16) * 16
    block_rows = pairs * SUB + info_rows
    block_len = taper_cols.shape[0]
    rows_here = block_len // epoch_count
    params = pltpu.CompilerParams(vmem_limit_bytes=VMEM_BYTES)
    turn_cos, turn_sin, second, last = tables

    slot_idx = jnp.arange(n_slots, dtype=jnp.int32)
    same_before = (slot_owner[:, None] == slot_owner[None, :]) & (
        slot_idx[None, :] < slot_idx[:, None]
    )
    slot_rank = jnp.sum(same_before.astype(jnp.int32), 1)
    hit = (slot_owner[None, None, :] == jnp.arange(tile_count, dtype=jnp.int32)[:, None, None]) & (
        slot_rank[None, None, :] == jnp.arange(info_rows, dtype=jnp.int32)[None, :, None]
    )
    fields = [
        jnp.sum(jnp.where(hit, f, 0), 2)
        for f in (
            jnp.ones_like(slot_owner),
            row_offsets[0],
            col_offsets[0] // LANES,
            col_offsets[0] % LANES,
            slot_idx,
        )
    ]
    source = fields[4][:, :capacity].reshape(-1)
    info = jnp.pad(jnp.stack(fields[:4], -1), ((0, 0), (0, 0), (0, LANES - 4))).astype(jnp.bfloat16)
    data = jnp.concatenate([coords[0], samples[0].astype(jnp.float32)], 1)

    tile_sems = pltpu.SemaphoreType.DMA((tile_count,))
    epoch_sems = pltpu.SemaphoreType.DMA(((epoch_count - 1) * tile_count,))
    got, others = pl.pallas_call(
        functools.partial(grid_kernel, pairs, tile_count, epoch_count),
        out_shape=[
            jax.ShapeDtypeStruct((n * tile_count, block_rows, LANES), jnp.bfloat16)
            for n in (1, epoch_count - 1)
        ],
        in_specs=smem(1) + vmem(2),
        out_specs=vmem(2),
        scratch_shapes=[
            pltpu.VMEM((tile_count, block_rows, LANES), jnp.bfloat16),
            tile_sems,
            tile_sems,
            epoch_sems,
            epoch_sems,
        ],
        compiler_params=pltpu.CompilerParams(
            vmem_limit_bytes=VMEM_BYTES, collective_id=1, has_side_effects=True
        ),
        name="grid_slots",
    )(source, data, info)
    spare = rows_here + 2 * SUB
    lane_blocks = tile_count * block_len // LANES

    def places(pool):
        table = pool[:, pairs * SUB : pairs * SUB + capacity, :4].astype(jnp.int32)
        valid = table[:, :, 0] > 0
        counts = jnp.sum(table[:, :, 0].reshape(-1, tile_count * capacity), 1)
        weight = jnp.repeat(1.0 / jnp.maximum(counts, 1).astype(jnp.float32), tile_count)
        first_row = table[:, :, 1] - epoch_index * rows_here + SUB
        inside = valid & (first_row > 0) & (first_row < rows_here + SUB)
        place_row = jnp.where(inside, first_row, spare).reshape(-1)
        return place_row, table[:, :, 2].reshape(-1), table[:, :, 3].reshape(-1), weight, pool

    acc = pltpu.VMEM((2, lane_blocks + 1, spare + SUB, LANES), jnp.float32)
    band = pl.pallas_call(
        functools.partial(place_kernel, pairs),
        out_shape=jax.ShapeDtypeStruct((2, lane_blocks, rows_here, LANES), jnp.bfloat16),
        in_specs=smem(4) + vmem(1),
        out_specs=vmem(1)[0],
        scratch_shapes=[acc],
        compiler_params=params,
        cost_estimate=pl.CostEstimate(flops=8 * 10**9, bytes_accessed=10**7, transcendentals=0),
        name="place_subgrids",
    )(*places(got))

    width = min(LANES, block_len)
    chunks = block_len // width
    sent = pl.pallas_call(
        functools.partial(rows_kernel, pairs),
        out_shape=[
            jax.ShapeDtypeStruct((tile_count, rows_here, 2 * width), jnp.bfloat16)
            for _ in range(chunks)
        ],
        in_specs=smem(4) + vmem(5),
        out_specs=vmem(chunks),
        scratch_shapes=[acc, pltpu.VMEM((tile_count, rows_here, 2 * block_len), jnp.bfloat16)],
        compiler_params=params,
        name="row_sections",
    )(*places(others), band, jnp.asarray(turn_cos), jnp.asarray(turn_sin), jnp.asarray(second))

    last_here = lax.dynamic_index_in_dim(jnp.asarray(last), epoch_index, 0, keepdims=False)
    kept = tile_count // epoch_count
    shares_shape = (chunks, epoch_count - 1, kept, block_len, width)
    tile_sems = pltpu.SemaphoreType.DMA((chunks * tile_count,))
    epoch_sems = pltpu.SemaphoreType.DMA((chunks * (epoch_count - 1) * kept,))
    sums = pl.pallas_call(
        functools.partial(columns_kernel, tile_count, epoch_count, chunks),
        out_shape=[
            jax.ShapeDtypeStruct((kept, block_len, width), jnp.float32) for _ in range(chunks)
        ],
        in_specs=vmem(chunks + 1),
        out_specs=vmem(chunks),
        scratch_shapes=[
            pltpu.VMEM((chunks, tile_count, rows_here, 2 * width), jnp.bfloat16),
            pltpu.VMEM((tile_count, 2 * rows_here, width), jnp.bfloat16),
            pltpu.VMEM(shares_shape, jnp.bfloat16),
            pltpu.VMEM(shares_shape, jnp.bfloat16),
            tile_sems,
            tile_sems,
            epoch_sems,
            epoch_sems,
            pltpu.SemaphoreType.DMA((chunks,)),
        ],
        compiler_params=pltpu.CompilerParams(
            vmem_limit_bytes=VMEM_BYTES, collective_id=0, has_side_effects=True
        ),
        name="columns",
    )(*sent, last_here)
    image_sum = jnp.concatenate(sums, 2)
    image_scale = math.sqrt(n_slots) / (64.0 * tile_count * math.sqrt(epoch_count))
    return image_sum * (image_scale * taper_rows)[:, :, None] * taper_cols[None, None, :]


def solution(mesh):
    placed = (
        P("epoch", "tile"),
        P("epoch", "tile"),
        P("epoch", "tile"),
        P("epoch", "tile", None, None),
        P("epoch", "tile", None, None),
        P("epoch", None),
        P("tile"),
    )

    def whole(owners, row_offsets, col_offsets, samples, coords, taper_rows, taper_cols):
        tables = make_tables(
            mesh.shape["tile"], mesh.shape["epoch"], taper_cols.shape[0] // mesh.shape["tile"]
        )
        return jax.shard_map(
            functools.partial(body, tables),
            mesh=mesh,
            in_specs=placed,
            out_specs=P("epoch", None, "tile"),
            check_vma=False,
        )(owners, row_offsets, col_offsets, samples, coords, taper_rows, taper_cols)

    return whole
```
